32 devices in a mesh: groups: 2 (over y), gy: 4 (over z), gx: 2 (over x), gz: 2 (over core).
Axes of the slice: x: 2, y: 2, z: 4, core: 2. Of those that a mesh axis runs over, the one named last changes fastest.
Arguments:
- charge_density: float32 [32, 32, 256], P(('groups', 'gx'), 'gy', 'gz'), parts along dimension 0, may hold values from -8 to 8
- permittivity: float32 [32, 32, 256], P(('groups', 'gx'), 'gy', 'gz'), parts along dimension 0, may hold values from 1 to 78
- ion_centers: float32 [4, 4, 2, 3, 4, 8], P(('groups', 'gx'), 'gy', 'gz'), parts along dimension 0, may hold values from -1 to 9
- ion_widths: float32 [4, 4, 2, 4, 8], P(('groups', 'gx'), 'gy', 'gz'), parts along dimension 0, may hold values from 1 to 2.5
- ion_charges: float32 [4, 4, 2, 4, 8], P(('groups', 'gx'), 'gy', 'gz'), parts along dimension 0, may hold values from -8 to 8
- block_counts: int32 [4, 4, 2, 4], P(('groups', 'gx'), 'gy', 'gz'), parts along dimension 0, may hold values from 0 to 8, as said below
- block_anchors: int32 [4, 4, 2, 3, 4, 8], P(('groups', 'gx'), 'gy', 'gz'), parts along dimension 0, may hold values from 0 to 120, as said below
Outputs:
- potential: float32 [32, 32, 256], P(('groups', 'gx'), 'gy', 'gz'), parts along dimension 0
The draws below stay inside these ranges and needn't reach their ends.
There are 2 independent parts, one for each index of `groups`. The reference program is written for one: setup_inputs(seed, part) draws one part's arguments, and reference() takes and returns one part's arrays. A program takes and returns all parts, laid end to end along the dimension named above; each array names one. Nothing has to cross between parts.
Inputs may be any that keep to these rules, and one draw needn't show every extreme that they name: `block_counts`: some brick rows, at least one, receive 8 live entries from every brick; the others fewer. `block_anchors`: component 0 lies in 0 to 0, component 1 in 0 to 0, component 2 in 0 to 120, so each block lies inside its brick.
All inputs are finite; a program needn't handle non-finite values.
Results may differ from the reference program's by a relative error of at most 0.0003.
Values may be sent and summed in bfloat16 or wider, within the bound.
A program may use at most 64 MiB of HBM per device.

```python
import math
import jax
import jax.numpy as jnp
from jax import lax

CX = 8
CY = 8
CZ = 128
PATCH = 8
CAP = 8
LEVELS = 4
NU_PRE = 1
NU_POST = 1
NU_COARSE = 8
NX = 16
NY = 32
NZ = 256
N_GY = 4
N_GX = 2
N_GZ = 2


def draw_charge_density(key, part):
    key = jax.random.fold_in(key, 11)
    first_key = jax.random.fold_in(key, 0)
    normal_part = jax.random.normal(first_key, (NX, NY, NZ), jnp.float32)
    values = normal_part
    return jnp.clip(values, -8.0, 8.0)


def draw_block_counts(key, part):
    key = jax.random.fold_in(key, 12)
    first_key, second_key = jax.random.split(key)
    ranking = jax.random.permutation(first_key, N_GY)
    crowded = ranking < max(1, N_GY // 4)
    sparse = jax.random.randint(second_key, (N_GX, N_GY, N_GZ, N_GY), 0, CAP // 2 + 1)
    return jnp.where(crowded[None, None, None, :], CAP, sparse).astype(jnp.int32)


def draw_block_anchors(key, part):
    key = jax.random.fold_in(key, 13)
    keys = jax.random.split(key, 3)
    shape_one = (N_GX, N_GY, N_GZ, 1, N_GY, CAP)
    first = jax.random.randint(keys[0], shape_one, 0, CX - PATCH + 1)
    second = jax.random.randint(keys[1], shape_one, 0, CY - PATCH + 1)
    third = jax.random.randint(keys[2], shape_one, 0, CZ - PATCH + 1)
    return jnp.concatenate([first, second, third], axis=3).astype(jnp.int32)


def shard_levels(own_key, shape, shards, smallest, largest):
    def one(axis_at, blocks):
        heights = jax.random.uniform(jax.random.fold_in(jax.random.fold_in(own_key, 6), axis_at), (blocks,), jnp.float32, smallest / len(shards), largest / len(shards))
        return jnp.repeat(jnp.exp(heights), shape[axis_at] // blocks).reshape((-1,) + (1,) * (len(shape) - axis_at - 1))

    factor_of = one(*shards[0])
    for cut in shards[1:]:
        factor_of = factor_of * one(*cut)
    return factor_of


def setup_inputs(seed: int = 0, part: int = 0) -> dict:
    streams_of = jax.random.split(jax.random.key(seed), 8)
    part_splits = jax.random.split(jax.random.fold_in(streams_of[7], part), 8)
    charge_density = draw_charge_density(jax.random.fold_in(jax.random.fold_in(streams_of[7], part), 71), part)
    permittivity = jnp.clip(jnp.exp(math.log(78.0) - 4.356709 * jax.random.uniform(part_splits[1], (NX, NY, NZ), jnp.float32) ** shard_levels(part_splits[1], (NX, NY, NZ), ((0, 2), (1, 4), (2, 2)), -0.2, 0.2)), 1.0, 78.0)
    ion_centers = jnp.clip(-1.0 + 10.0 * jax.random.uniform(part_splits[2], (N_GX, N_GY, N_GZ, 3, N_GY, CAP), jnp.float32) ** shard_levels(part_splits[2], (N_GX, N_GY, N_GZ, 3, N_GY, CAP), ((0, 2), (1, 4), (2, 2)), -0.2, 0.2), -1.0, 9.0)
    ion_widths = jnp.clip(jnp.exp(math.log(2.5) - 0.916290732 * jax.random.uniform(part_splits[3], (N_GX, N_GY, N_GZ, N_GY, CAP), jnp.float32) ** shard_levels(part_splits[3], (N_GX, N_GY, N_GZ, N_GY, CAP), ((0, 2), (1, 4), (2, 2)), -0.2, 0.2)), 1.0, 2.5)
    ion_charges = jnp.clip(jax.random.uniform(part_splits[4], (N_GX, N_GY, N_GZ, N_GY, CAP), jnp.float32, -8.0, 8.0) * shard_levels(part_splits[4], (N_GX, N_GY, N_GZ, N_GY, CAP), ((0, 2), (1, 4), (2, 2)), -0.4, 0.0), -8.0, 8.0)
    block_counts = draw_block_counts(jax.random.fold_in(jax.random.fold_in(streams_of[7], part), 71), part)
    block_anchors = draw_block_anchors(jax.random.fold_in(jax.random.fold_in(streams_of[7], part), 71), part)
    return dict(charge_density=charge_density, permittivity=permittivity, ion_centers=ion_centers, ion_widths=ion_widths, ion_charges=ion_charges, block_counts=block_counts, block_anchors=block_anchors)


four_pi = 4.0 * math.pi
relax_weight = 2.0 / 3.0
gauss_norm = (2.0 * math.pi) ** 1.5


def gaussian_blocks(centre_x, centre_y, centre_z, spread, charge):
    positions = jnp.arange(PATCH, dtype=jnp.float32)
    decay_rate = 0.5 / (spread * spread)
    profile_x = jnp.exp(-((positions[None, :] - centre_x[:, None]) ** 2) * decay_rate[:, None])
    profile_y = jnp.exp(-((positions[None, :] - centre_y[:, None]) ** 2) * decay_rate[:, None])
    profile_z = jnp.exp(-((positions[None, :] - centre_z[:, None]) ** 2) * decay_rate[:, None])
    amplitude = charge / (gauss_norm * spread * spread * spread)
    blocks_out = amplitude[:, None, None, None] * profile_x[:, :, None, None] * profile_y[:, None, :, None] * profile_z[:, None, None, :]
    return blocks_out.reshape(centre_x.shape[0], PATCH * PATCH * PATCH)


def face_weights(padded):
    centre = padded[1:-1, 1:-1, 1:-1]
    weights = (0.5 * (centre + padded[2:, 1:-1, 1:-1]), 0.5 * (centre + padded[:-2, 1:-1, 1:-1]),
               0.5 * (centre + padded[1:-1, 2:, 1:-1]), 0.5 * (centre + padded[1:-1, :-2, 1:-1]),
               0.5 * (centre + padded[1:-1, 1:-1, 2:]), 0.5 * (centre + padded[1:-1, 1:-1, :-2]))
    weight_sum = weights[0] + weights[1] + weights[2] + weights[3] + weights[4] + weights[5]
    return weights, weight_sum


def apply_operator(padded, weights, weight_sum, spacing_factor):
    centre = padded[1:-1, 1:-1, 1:-1]
    beside = weights[0] * padded[2:, 1:-1, 1:-1] + weights[1] * padded[:-2, 1:-1, 1:-1]
    beside = beside + weights[2] * padded[1:-1, 2:, 1:-1] + weights[3] * padded[1:-1, :-2, 1:-1]
    beside = beside + weights[4] * padded[1:-1, 1:-1, 2:] + weights[5] * padded[1:-1, 1:-1, :-2]
    return spacing_factor * (weight_sum * centre - beside)


def restrict_mean(values):
    size_a, size_b, size_c = values.shape
    return values.reshape(size_a // 2, 2, size_b // 2, 2, size_c // 2, 2).mean(axis=(1, 3, 5))


def prolong(values):
    return jnp.repeat(jnp.repeat(jnp.repeat(values, 2, 0), 2, 1), 2, 2)


def zero_pad(values):
    return jnp.pad(values, 1)


def smooth_sweeps(potential, source, weights, weight_sum, diagonal, spacing_factor, sweeps):
    for sweep_index in range(sweeps):
        applied = apply_operator(zero_pad(potential), weights, weight_sum, spacing_factor)
        potential = potential + relax_weight * (source - applied) / diagonal
    return potential


def multigrid_level(source, permittivity, level_index):
    spacing_factor = 1.0 / 4.0 ** level_index
    weights, weight_sum = face_weights(zero_pad(permittivity))
    diagonal = spacing_factor * weight_sum
    potential = jnp.zeros_like(source)
    if level_index == LEVELS - 1:
        return smooth_sweeps(potential, source, weights, weight_sum, diagonal, spacing_factor, NU_COARSE)
    potential = smooth_sweeps(potential, source, weights, weight_sum, diagonal, spacing_factor, NU_PRE)
    residual = source - apply_operator(zero_pad(potential), weights, weight_sum, spacing_factor)
    correction = multigrid_level(restrict_mean(residual), restrict_mean(permittivity), level_index + 1)
    potential = potential + prolong(correction)
    return smooth_sweeps(potential, source, weights, weight_sum, diagonal, spacing_factor, NU_POST)


def reference(charge_density, permittivity, ion_centers, ion_widths, ion_charges, block_counts, block_anchors):
    slot_index = jnp.arange(CAP, dtype=jnp.int32)
    live_slot = (slot_index[None, None, None, None, :] < block_counts[..., None]).reshape(-1)
    blocks_out = gaussian_blocks(ion_centers[:, :, :, 0].reshape(-1), ion_centers[:, :, :, 1].reshape(-1),
                                 ion_centers[:, :, :, 2].reshape(-1), ion_widths.reshape(-1), ion_charges.reshape(-1))
    rounded = lax.optimization_barrier(blocks_out.astype(jnp.bfloat16)).astype(jnp.float32)
    deposits = jnp.where(live_slot[:, None], rounded, 0.0)
    brick_x = jnp.arange(N_GX, dtype=jnp.int32)[:, None, None, None, None] * CX
    brick_y = jnp.arange(N_GY, dtype=jnp.int32)[None, None, None, :, None] * CY
    brick_z = jnp.arange(N_GZ, dtype=jnp.int32)[None, None, :, None, None] * CZ
    corner_x = brick_x + block_anchors[:, :, :, 0]
    corner_y = brick_y + block_anchors[:, :, :, 1]
    corner_z = brick_z + block_anchors[:, :, :, 2]
    anchor_flat = ((corner_x * NY + corner_y) * NZ + corner_z).reshape(-1).astype(jnp.int32)
    patch_steps = jnp.arange(PATCH, dtype=jnp.int32)
    offsets = ((patch_steps[:, None, None] * NY + patch_steps[None, :, None]) * NZ + patch_steps[None, None, :]).reshape(-1)
    targets = (anchor_flat[:, None] + offsets[None, :]).astype(jnp.int32)
    density = charge_density.reshape(-1).at[targets.reshape(-1)].add(deposits.reshape(-1)).reshape(NX, NY, NZ)
    source = four_pi * density
    return multigrid_level(source, permittivity, 0)
```

```python
import functools
import math

import jax
import jax.numpy as jnp
from jax import lax
from jax.experimental import pallas as pl
from jax.experimental.pallas import tpu as pltpu
from jax.sharding import PartitionSpec as P

PATCH = 8
CAP = 8
NU_COARSE = 8
MESH = pl.DeviceIdType.MESH

four_pi = 4.0 * math.pi
relax_weight = 2.0 / 3.0
gauss_norm = (2.0 * math.pi) ** 1.5


def iota(shape, dim):
    return lax.broadcasted_iota(jnp.int32, shape, dim)


def each(count, body):
    if count <= 16:
        for k in range(1, count):
            body(k)
    else:
        lax.fori_loop(1, count, lambda k, c: (body(k), c)[1], 0)


def rolled(values, step, dim):
    return pltpu.roll(values, step % values.shape[dim], dim)


def pair_sum_z(values, step):
    low = (iota(values.shape, 2) // step) % 2 == 0
    return values + jnp.where(low, rolled(values, -step, 2), rolled(values, step, 2))


def pair_sum_x(values):
    a, b, c = values.shape
    v = values.reshape(a // 2, 2, b, c)
    return v[:, 0] + v[:, 1]


def repeat_x(values):
    a, b, c = values.shape
    return jnp.broadcast_to(values[:, None], (a, 2, b, c)).reshape(2 * a, b, c)


def shifted_x(values, step):
    zero = jnp.zeros_like(values[:1])
    if step > 0:
        return jnp.concatenate([values[1:], zero], 0)
    return jnp.concatenate([zero, values[:-1]], 0)


class Coarse:
    def __init__(self, eps, level, sy, sz):
        self.sy, self.sz = sy, sz
        self.spacing = 1.0 / 4.0**level
        y, z = iota(eps.shape, 1), iota(eps.shape, 2)
        ny, nz = eps.shape[1], eps.shape[2]
        xp, xm = shifted_x(eps, 1), shifted_x(eps, -1)
        in_y, in_z = y < ny - sy, z < nz - sz
        yp = jnp.where(in_y, rolled(eps, -sy, 1), 0.0)
        ym = jnp.where(y >= sy, rolled(eps, sy, 1), 0.0)
        zp = jnp.where(in_z, rolled(eps, -sz, 2), 0.0)
        zm = jnp.where(z >= sz, rolled(eps, sz, 2), 0.0)
        weight_sum = 0.5 * (6.0 * eps + xp + xm + yp + ym + zp + zm)
        self.inverse = (relax_weight / self.spacing) / weight_sum
        self.wx = 0.5 * (eps + xp)
        self.wy = jnp.where(in_y, 0.5 * (eps + yp), 0.0)
        self.wz = jnp.where(in_z, 0.5 * (eps + zp), 0.0)

    def beside(self, f):
        out = self.wx * shifted_x(f, 1) + shifted_x(self.wx * f, -1)
        out += self.wy * rolled(f, -self.sy, 1) + rolled(self.wy * f, self.sy, 1)
        out += self.wz * rolled(f, -self.sz, 2) + rolled(self.wz * f, self.sz, 2)
        return self.spacing * out

    def first(self, g):
        return self.inverse * g

    def residual_of_first(self, g, f):
        return (1.0 / 3.0) * g + self.beside(f)

    def sweep(self, g, f):
        return (1.0 / 3.0) * f + self.inverse * (g + self.beside(f))


def around(values, halo):
    (xl, xh), (yl, yh), (zl, zh) = halo
    y, z = iota(values.shape, 1), iota(values.shape, 2)
    ny, nz = values.shape[1], values.shape[2]
    shape = values.shape
    return (
        jnp.concatenate([values[1:], xh[None]], 0),
        jnp.concatenate([xl[None], values[:-1]], 0),
        jnp.where(y == ny - 1, jnp.broadcast_to(yh, shape), rolled(values, -1, 1)),
        jnp.where(y == 0, jnp.broadcast_to(yl, shape), rolled(values, 1, 1)),
        jnp.where(z == nz - 1, rolled(zh, -1, 2), rolled(values, -1, 2)),
        jnp.where(z == 0, rolled(zl, 1, 2), rolled(values, 1, 2)),
    )


def kernel(
    sizes,
    charge_ref, eps_ref, centers_ref, widths_ref, charges_ref, counts_ref, anchors_ref,
    out_ref,
    f_ref, hx_ref, hy_ref, hz_ref, sy_ref, pairs_ref, gather_ref, ions_out, ions_in, whole1, half2, up1, up0,
    face_send, face_recv, gather_send, gather_recv, ion_send, ion_recv,
):
    ngx, ngy, ngz = sizes
    cx, cy, cz = charge_ref.shape
    bx, by = cx // 2, cy // 2
    n = ngx * ngy * ngz
    gx, gy, gz = lax.axis_index("gx"), lax.axis_index("gy"), lax.axis_index("gz")
    me = (gx * ngy + gy) * ngz + gz

    def peer(k):
        at = (me + k) % n
        return {"gx": at // (ngy * ngz), "gy": (at // ngz) % ngy, "gz": at % ngz}

    barrier = pltpu.get_barrier_semaphore()
    each(n, lambda k: pl.semaphore_signal(barrier, inc=1, device_id=peer(k), device_id_type=MESH))

    axes = (("gx", gx, ngx), ("gy", gy, ngy), ("gz", gz, ngz))
    halos = (hx_ref, hy_ref, hz_ref)
    for axis in range(3):
        name, at, count = axes[axis]
        for side, missing in ((0, at == 0), (1, at == count - 1)):
            @pl.when(missing)
            def _(axis=axis, side=side):
                for kind in range(2):
                    buffer = halos[axis].at[kind, side]
                    buffer[...] = jnp.zeros(buffer.shape, jnp.float32)

    def face_copy(kind, axis, side, source):
        name, at, count = axes[axis]
        target = at + 1 if side == 0 else at - 1
        index = (kind * 3 + axis) * 2 + side
        return pltpu.make_async_remote_copy(
            src_ref=source, dst_ref=halos[axis].at[kind, side],
            send_sem=face_send.at[index], recv_sem=face_recv.at[index],
            device_id={name: target}, device_id_type=MESH)

    def face_sources(kind, field):
        return (
            (field.at[cx - 1], field.at[0]),
            (sy_ref.at[kind, 0], sy_ref.at[kind, 1]),
            (field, field),
        )

    def send_faces(kind, field):
        sy_ref[kind, 0] = field[:, cy - 1 : cy, :]
        sy_ref[kind, 1] = field[:, 0:1, :]
        sources = face_sources(kind, field)
        for axis in range(3):
            at, count = axes[axis][1:]
            for side in range(2):
                @pl.when((at < count - 1) if side == 0 else (at > 0))
                def _(axis=axis, side=side):
                    face_copy(kind, axis, side, sources[axis][side]).start()

    def wait_faces(kind, field, sent):
        sources = face_sources(kind, field)
        for axis in range(3):
            at, count = axes[axis][1:]
            for side in range(2):
                up = (side == 0) == sent
                @pl.when((at < count - 1) if up else (at > 0))
                def _(axis=axis, side=side):
                    copy = face_copy(kind, axis, side, sources[axis][side])
                    copy.wait_send() if sent else copy.wait_recv()

    def gather_copy(kind, k):
        return pltpu.make_async_remote_copy(
            src_ref=gather_ref.at[kind, me], dst_ref=gather_ref.at[kind, me],
            send_sem=gather_send.at[kind, k], recv_sem=gather_recv.at[kind, k],
            device_id=peer(k), device_id_type=MESH)

    def ion_copy(k):
        to = (gy + k) % ngy
        return pltpu.make_async_remote_copy(
            src_ref=ions_out.at[to], dst_ref=ions_in.at[gy],
            send_sem=ion_send.at[k], recv_sem=ion_recv.at[k],
            device_id={"gy": to}, device_id_type=MESH)

    def restrict(values):
        pairs_ref[...] = pair_sum_z(pair_sum_x(values), 1)
        return 0.125 * (pairs_ref[:, pl.ds(0, by, stride=2), :] + pairs_ref[:, pl.ds(1, by, stride=2), :])

    def assemble(kind):
        for a in range(ngx):
            for b in range(ngy):
                for c in range(ngz):
                    whole1[a * bx : (a + 1) * bx, b * by : (b + 1) * by, c * cz : (c + 1) * cz] = gather_ref[
                        kind, (a * ngy + b) * ngz + c]
        return whole1[...]

    eps = eps_ref[...]
    gather_ref[0, me] = restrict(eps)
    counts = counts_ref[...]
    for d in range(ngy):
        for c in range(3):
            ions_out[d, c : c + 1, 0:CAP] = centers_ref[c, d : d + 1, :]
        ions_out[d, 3:4, 0:CAP] = widths_ref[d : d + 1, :]
        live = iota((1, CAP), 1) < jnp.broadcast_to(counts[:, d : d + 1], (1, CAP))
        ions_out[d, 4:5, 0:CAP] = jnp.where(live, charges_ref[d : d + 1, :], 0.0)
        ions_out[d, 5:6, 0:CAP] = anchors_ref[2, d : d + 1, :].astype(jnp.float32)
        ions_out[d, 6:8, 0:CAP] = jnp.zeros((2, CAP), jnp.float32)
        ions_out[d, :, CAP:] = jnp.ones((8, 128 - CAP), jnp.float32)
    ions_in[gy] = ions_out[gy]
    up0[...] = jnp.zeros_like(up0)

    pl.semaphore_wait(barrier, n - 1)
    each(ngy, lambda k: ion_copy(k).start())
    send_faces(0, eps_ref)
    each(n, lambda k: gather_copy(0, k).start())

    each(ngy, lambda k: ion_copy(k).wait_recv())

    def deposit(source, density):
        tile = ions_in[source]
        lines = tile.T[0:CAP]
        u, v, s, q = tile[0:1], tile[1:2], tile[3:4], tile[4:5]
        decay = 0.5 / (s * s)
        amplitude = q / (gauss_norm * s * s * s)
        j = iota((cy, 128), 0).astype(jnp.float32)
        along_y = jnp.exp(-((j - v) ** 2) * decay)
        flat = jnp.stack(
            [(amplitude * jnp.exp(-((float(i) - u) ** 2) * decay)) * along_y for i in range(cx)])
        w, spread, anchor = lines[:, 2:3], lines[:, 3:4], lines[:, 5:6]
        position = iota((CAP, cz), 1).astype(jnp.float32) - anchor
        along_z = jnp.exp(-((position - w) ** 2) * (0.5 / (spread * spread)))
        along_z = jnp.where((position >= 0.0) & (position < float(PATCH)), along_z, 0.0)
        for e in range(CAP):
            block = flat[:, :, e : e + 1] * along_z[None, e : e + 1, :]
            density += block.astype(jnp.bfloat16).astype(jnp.float32)
        return density

    density = charge_ref[...]
    if ngy <= 4:
        for source in range(ngy):
            density = deposit(source, density)
    else:
        density = lax.fori_loop(0, ngy, deposit, density)
    g = four_pi * density

    wait_faces(0, eps_ref, False)

    def halo(kind):
        return tuple((buffer[kind, 0], buffer[kind, 1]) for buffer in halos)

    eps_around = around(eps, halo(0))
    weight_sum = 0.5 * (6.0 * eps + sum(eps_around[1:], eps_around[0]))
    weights = [0.5 * (eps + other) for other in eps_around]
    inverse = relax_weight / weight_sum
    f = inverse * g
    f_ref[...] = f
    send_faces(1, f_ref)

    each(n, lambda k: gather_copy(0, k).wait_recv())
    nx1, ny1 = whole1.shape[:2]

    def down_y(values):
        rows = ny1 // 2
        parts = []
        for c in range(ngz):
            half2[c] = values[:, :, c * cz : (c + 1) * cz]
            parts.append(half2[c, :, pl.ds(0, rows, stride=2), :] + half2[c, :, pl.ds(1, rows, stride=2), :])
        return jnp.concatenate(parts, 2)

    def pair_sum_y(values):
        low = iota(values.shape, 1) % 2 == 0
        return values + jnp.where(low, rolled(values, -1, 1), rolled(values, 1, 1))

    def restrict_1(values):
        return 0.125 * down_y(pair_sum_z(pair_sum_x(values), 2))

    def restrict_2(values):
        return 0.125 * pair_sum_y(pair_sum_z(pair_sum_x(values), 4))

    eps1 = assemble(0)
    eps2 = restrict_1(eps1)
    eps3 = restrict_2(eps2)
    level1, level2, level3 = Coarse(eps1, 1, 1, 2), Coarse(eps2, 2, 1, 4), Coarse(eps3, 3, 2, 8)

    wait_faces(1, f_ref, False)

    def beside(values, halo_values):
        total = None
        for weight, other in zip(weights, around(values, halo_values)):
            total = weight * other if total is None else total + weight * other
        return total

    f_halo = halo(1)
    gather_ref[1, me] = restrict((1.0 / 3.0) * g + beside(f, f_halo))
    each(n, lambda k: gather_copy(1, k).start())
    each(n, lambda k: gather_copy(1, k).wait_recv())

    g1 = assemble(1)
    f1 = level1.first(g1)
    g2 = restrict_1(level1.residual_of_first(g1, f1))
    f2 = level2.first(g2)
    g3 = restrict_2(level2.residual_of_first(g2, f2))
    f3 = level3.first(g3)
    for _ in range(NU_COARSE - 1):
        f3 = level3.sweep(g3, f3)
    f2 = level2.sweep(g2, f2 + repeat_x(f3))
    fine2 = repeat_x(f2)
    for c in range(ngz):
        for odd in range(2):
            up1[c, :, pl.ds(odd, ny1 // 2, stride=2), :] = fine2[:, :, c * cz : (c + 1) * cz]
    f1 = level1.sweep(g1, f1 + jnp.concatenate([up1[c] for c in range(ngz)], 2))
    for c in range(ngz):
        for odd in range(2):
            up0[c + 1, 1 : nx1 + 1, pl.ds(cy + odd, ny1, stride=2), :] = f1[:, :, c * cz : (c + 1) * cz]

    def part(dx, lx, dy, dz):
        return up0[gz + dz, pl.ds(gx * bx + dx, lx), pl.ds(pl.multiple_of((gy + dy) * cy, cy), cy), :]

    (xl, xh), (yl, yh), (zl, zh) = f_halo
    f = f + repeat_x(part(1, bx, 1, 1))
    f_halo = (
        (xl + part(0, 1, 1, 1)[0], xh + part(bx + 1, 1, 1, 1)[0]),
        (yl + repeat_x(part(1, bx, 0, 1)[:, cy - 1 : cy, :]), yh + repeat_x(part(1, bx, 2, 1)[:, 0:1, :])),
        (zl + repeat_x(part(1, bx, 1, 0)), zh + repeat_x(part(1, bx, 1, 2))),
    )
    out_ref[...] = (1.0 / 3.0) * f + inverse * (g + beside(f, f_halo))

    each(ngy, lambda k: ion_copy(k).wait_send())
    wait_faces(0, eps_ref, True)
    wait_faces(1, f_ref, True)
    each(n, lambda k: gather_copy(0, k).wait_send())
    each(n, lambda k: gather_copy(1, k).wait_send())


def solution(mesh):
    ngx, ngy, ngz = mesh.shape["gx"], mesh.shape["gy"], mesh.shape["gz"]

    def per_device(charge_density, permittivity, ion_centers, ion_widths, ion_charges, block_counts, block_anchors):
        cx, cy, cz = charge_density.shape
        n = ngx * ngy * ngz
        nx1, ny1 = ngx * cx // 2, ngy * cy // 2
        f32 = jnp.float32
        dma = pltpu.SemaphoreType.DMA
        return pl.pallas_call(
            functools.partial(kernel, (ngx, ngy, ngz)),
            out_shape=jax.ShapeDtypeStruct((cx, cy, cz), f32),
            in_specs=[pl.BlockSpec(memory_space=pltpu.VMEM)] * 7,
            out_specs=pl.BlockSpec(memory_space=pltpu.VMEM),
            scratch_shapes=[
                pltpu.VMEM((cx, cy, cz), f32),
                pltpu.VMEM((2, 2, cy, cz), f32),
                pltpu.VMEM((2, 2, cx, 1, cz), f32),
                pltpu.VMEM((2, 2, cx, cy, cz), f32),
                pltpu.VMEM((2, 2, cx, 1, cz), f32),
                pltpu.VMEM((cx // 2, cy, cz), f32),
                pltpu.VMEM((2, n, cx // 2, cy // 2, cz), f32),
                pltpu.VMEM((ngy, 8, 128), f32),
                pltpu.VMEM((ngy, 8, 128), f32),
                pltpu.VMEM((nx1, ny1, ngz * cz), f32),
                pltpu.VMEM((ngz, nx1 // 2, ny1, cz), f32),
                pltpu.VMEM((ngz, nx1, ny1, cz), f32),
                pltpu.VMEM((ngz + 2, nx1 + 2, (ngy + 2) * cy, cz), f32),
                dma((12,)), dma((12,)), dma((2, n)), dma((2, n)), dma((ngy,)), dma((ngy,)),
            ],
            compiler_params=pltpu.CompilerParams(
                collective_id=0, has_side_effects=True, vmem_limit_bytes=48 * 1024 * 1024),
        )(
            charge_density,
            permittivity,
            ion_centers.reshape(3, ngy, CAP),
            ion_widths.reshape(ngy, CAP),
            ion_charges.reshape(ngy, CAP),
            block_counts.reshape(1, ngy),
            block_anchors.reshape(3, ngy, CAP),
        )

    field = P(("groups", "gx"), "gy", "gz")
    return jax.shard_map(
        per_device, mesh=mesh, in_specs=(field,) * 7, out_specs=field, check_vma=False)
```

```python
import functools
import math

import jax
import jax.numpy as jnp
from jax import lax
from jax.experimental import pallas as pl
from jax.experimental.pallas import tpu as pltpu
from jax.sharding import PartitionSpec as P

PATCH = 8
CAP = 8
NU_COARSE = 8
MESH = pl.DeviceIdType.MESH

four_pi = 4.0 * math.pi
relax_weight = 2.0 / 3.0
gauss_norm = (2.0 * math.pi) ** 1.5


def iota(shape, dim):
    return lax.broadcasted_iota(jnp.int32, shape, dim)


def each(count, body):
    if count <= 16:
        for k in range(1, count):
            body(k)
    else:
        lax.fori_loop(1, count, lambda k, c: (body(k), c)[1], 0)


def rolled(values, step, dim):
    return pltpu.roll(values, step % values.shape[dim], dim)


def pair_sum_z(values, step):
    low = (iota(values.shape, 2) // step) % 2 == 0
    return values + jnp.where(low, rolled(values, -step, 2), rolled(values, step, 2))


def pair_sum_x(values):
    a, b, c = values.shape
    v = values.reshape(a // 2, 2, b, c)
    return v[:, 0] + v[:, 1]


def repeat_x(values):
    a, b, c = values.shape
    return jnp.broadcast_to(values[:, None], (a, 2, b, c)).reshape(2 * a, b, c)


def shifted_x(values, step):
    zero = jnp.zeros_like(values[:1])
    if step > 0:
        return jnp.concatenate([values[1:], zero], 0)
    return jnp.concatenate([zero, values[:-1]], 0)


def packed(values):
    a, b, c = values.shape
    v = values.reshape(a // 2, 2, b, c)
    return jnp.where(iota((a // 2, b, c), 2) % 2 == 0, v[:, 0], v[:, 1])


def unpacked(values):
    a, b, c = values.shape
    even = iota(values.shape, 2) % 2 == 0
    first = jnp.where(even, values, rolled(values, 1, 2))
    second = jnp.where(even, rolled(values, -1, 2), values)
    return jnp.stack([first, second], 1).reshape(2 * a, b, c)


class Coarse:
    def __init__(self, eps, level, sy, sz):
        self.sy, self.sz = sy, sz
        self.spacing = 1.0 / 4.0**level
        y, z = iota(eps.shape, 1), iota(eps.shape, 2)
        ny, nz = eps.shape[1], eps.shape[2]
        xp, xm = shifted_x(eps, 1), shifted_x(eps, -1)
        in_y, in_z = y < ny - sy, z < nz - sz
        yp = jnp.where(in_y, rolled(eps, -sy, 1), 0.0)
        ym = jnp.where(y >= sy, rolled(eps, sy, 1), 0.0)
        zp = jnp.where(in_z, rolled(eps, -sz, 2), 0.0)
        zm = jnp.where(z >= sz, rolled(eps, sz, 2), 0.0)
        weight_sum = 0.5 * (6.0 * eps + xp + xm + yp + ym + zp + zm)
        self.inverse = (relax_weight / self.spacing) / weight_sum
        self.wx = 0.5 * (eps + xp)
        self.wy = jnp.where(in_y, 0.5 * (eps + yp), 0.0)
        self.wz = jnp.where(in_z, 0.5 * (eps + zp), 0.0)

    def beside(self, f):
        out = self.wx * shifted_x(f, 1) + shifted_x(self.wx * f, -1)
        out += self.wy * rolled(f, -self.sy, 1) + rolled(self.wy * f, self.sy, 1)
        out += self.wz * rolled(f, -self.sz, 2) + rolled(self.wz * f, self.sz, 2)
        return self.spacing * out

    def first(self, g):
        return self.inverse * g

    def residual_of_first(self, g, f):
        return (1.0 / 3.0) * g + self.beside(f)

    def sweep(self, g, f):
        return (1.0 / 3.0) * f + self.inverse * (g + self.beside(f))


def around(values, halo):
    (xl, xh), (yl, yh), (zl, zh) = halo
    y, z = iota(values.shape, 1), iota(values.shape, 2)
    ny, nz = values.shape[1], values.shape[2]
    shape = values.shape
    return (
        jnp.concatenate([values[1:], xh[None]], 0),
        jnp.concatenate([xl[None], values[:-1]], 0),
        jnp.where(y == ny - 1, jnp.broadcast_to(yh, shape), rolled(values, -1, 1)),
        jnp.where(y == 0, jnp.broadcast_to(yl, shape), rolled(values, 1, 1)),
        jnp.where(z == nz - 1, rolled(zh, -1, 2), rolled(values, -1, 2)),
        jnp.where(z == 0, rolled(zl, 1, 2), rolled(values, 1, 2)),
    )


def kernel(
    sizes,
    charge_in, eps_in, centers_in, widths_in, charges_in, counts_in, anchors_in,
    out_ref,
    charge_ref, eps_ref, centers_ref, widths_ref, charges_ref, counts_ref, anchors_ref, load_sem,
    f_ref, hx_ref, hy_ref, hz_ref, sy_ref, pairs_ref, gather_ref, ions_out, ions_in, whole1, half2, up1, up0,
    face_send, face_recv, gather_send, gather_recv, ion_send, ion_recv,
):
    ngx, ngy, ngz = sizes
    cx, cy, cz = charge_ref.shape
    bx, by, hx = cx // 2, cy // 2, cx // 4
    n = ngx * ngy * ngz
    gx, gy, gz = lax.axis_index("gx"), lax.axis_index("gy"), lax.axis_index("gz")
    me = (gx * ngy + gy) * ngz + gz

    def peer(k):
        at = (me + k) % n
        return {"gx": at // (ngy * ngz), "gy": (at // ngz) % ngy, "gz": at % ngz}

    loads = [
        pltpu.make_async_copy(source, target, load_sem.at[index])
        for index, (source, target) in enumerate((
            (eps_in, eps_ref), (counts_in, counts_ref), (centers_in, centers_ref), (widths_in, widths_ref),
            (charges_in, charges_ref), (anchors_in, anchors_ref), (charge_in, charge_ref)))
    ]
    for load in loads:
        load.start()
    barrier = pltpu.get_barrier_semaphore()
    each(n, lambda k: pl.semaphore_signal(barrier, inc=1, device_id=peer(k), device_id_type=MESH))

    axes = (("gx", gx, ngx), ("gy", gy, ngy), ("gz", gz, ngz))
    halos = (hx_ref, hy_ref, hz_ref)
    for axis in range(3):
        name, at, count = axes[axis]
        for side, missing in ((0, at == 0), (1, at == count - 1)):
            @pl.when(missing)
            def _(axis=axis, side=side):
                for kind in range(2):
                    buffer = halos[axis].at[kind, side]
                    buffer[...] = jnp.zeros(buffer.shape, jnp.float32)

    def face_copy(kind, axis, side, source):
        name, at, count = axes[axis]
        target = at + 1 if side == 0 else at - 1
        index = (kind * 3 + axis) * 2 + side
        return pltpu.make_async_remote_copy(
            src_ref=source, dst_ref=halos[axis].at[kind, side],
            send_sem=face_send.at[index], recv_sem=face_recv.at[index],
            device_id={name: target}, device_id_type=MESH)

    def face_sources(kind, field):
        return (
            (field.at[cx - 1], field.at[0]),
            (sy_ref.at[kind, 0], sy_ref.at[kind, 1]),
            (field, field),
        )

    def send_faces(kind, field):
        sy_ref[kind, 0] = field[:, cy - 1 : cy, :]
        sy_ref[kind, 1] = field[:, 0:1, :]
        sources = face_sources(kind, field)
        for axis in range(3):
            at, count = axes[axis][1:]
            for side in range(2):
                @pl.when((at < count - 1) if side == 0 else (at > 0))
                def _(axis=axis, side=side):
                    face_copy(kind, axis, side, sources[axis][side]).start()

    def wait_faces(kind, field, sent):
        sources = face_sources(kind, field)
        for axis in range(3):
            at, count = axes[axis][1:]
            for side in range(2):
                up = (side == 0) == sent
                @pl.when((at < count - 1) if up else (at > 0))
                def _(axis=axis, side=side):
                    copy = face_copy(kind, axis, side, sources[axis][side])
                    copy.wait_send() if sent else copy.wait_recv()

    def gather_copy(kind, k):
        return pltpu.make_async_remote_copy(
            src_ref=gather_ref.at[kind, me], dst_ref=gather_ref.at[kind, me],
            send_sem=gather_send.at[kind, k], recv_sem=gather_recv.at[kind, k],
            device_id=peer(k), device_id_type=MESH)

    def ion_copy(k):
        to = (gy + k) % ngy
        return pltpu.make_async_remote_copy(
            src_ref=ions_out.at[to], dst_ref=ions_in.at[gy],
            send_sem=ion_send.at[k], recv_sem=ion_recv.at[k],
            device_id={"gy": to}, device_id_type=MESH)

    def restrict(values):
        pairs_ref[...] = pair_sum_z(pair_sum_x(values), 1)
        return 0.125 * (pairs_ref[:, pl.ds(0, by, stride=2), :] + pairs_ref[:, pl.ds(1, by, stride=2), :])

    def assemble(kind):
        for a in range(ngx):
            for b in range(ngy):
                for c in range(ngz):
                    whole1[a * hx : (a + 1) * hx, b * by : (b + 1) * by, c * cz : (c + 1) * cz] = gather_ref[
                        kind, (a * ngy + b) * ngz + c]
        return unpacked(whole1[...])

    up0[...] = jnp.zeros_like(up0)
    loads[0].wait()
    eps = eps_ref[...]
    gather_ref[0, me] = packed(restrict(eps))
    for load in loads[1:6]:
        load.wait()
    counts = counts_ref[...]
    for d in range(ngy):
        for c in range(3):
            ions_out[d, c : c + 1, 0:CAP] = centers_ref[c, d : d + 1, :]
        ions_out[d, 3:4, 0:CAP] = widths_ref[d : d + 1, :]
        live = iota((1, CAP), 1) < jnp.broadcast_to(counts[:, d : d + 1], (1, CAP))
        ions_out[d, 4:5, 0:CAP] = jnp.where(live, charges_ref[d : d + 1, :], 0.0)
        ions_out[d, 5:6, 0:CAP] = anchors_ref[2, d : d + 1, :].astype(jnp.float32)
        ions_out[d, 6:8, 0:CAP] = jnp.zeros((2, CAP), jnp.float32)
        ions_out[d, :, CAP:] = jnp.ones((8, 128 - CAP), jnp.float32)
    ions_in[gy] = ions_out[gy]

    pl.semaphore_wait(barrier, n - 1)
    each(ngy, lambda k: ion_copy(k).start())
    send_faces(0, eps_ref)
    each(n, lambda k: gather_copy(0, k).start())

    each(ngy, lambda k: ion_copy(k).wait_recv())

    def deposit(source, density):
        tile = ions_in[source]
        lines = tile.T[0:CAP]
        u, v, s, q = tile[0:1], tile[1:2], tile[3:4], tile[4:5]
        decay = 0.5 / (s * s)
        amplitude = q / (gauss_norm * s * s * s)
        j = iota((cy, 128), 0).astype(jnp.float32)
        along_y = jnp.exp(-((j - v) ** 2) * decay)
        flat = jnp.stack(
            [(amplitude * jnp.exp(-((float(i) - u) ** 2) * decay)) * along_y for i in range(cx)])
        w, spread, anchor = lines[:, 2:3], lines[:, 3:4], lines[:, 5:6]
        position = iota((CAP, cz), 1).astype(jnp.float32) - anchor
        along_z = jnp.exp(-((position - w) ** 2) * (0.5 / (spread * spread)))
        along_z = jnp.where((position >= 0.0) & (position < float(PATCH)), along_z, 0.0)
        for e in range(CAP):
            block = flat[:, :, e : e + 1] * along_z[None, e : e + 1, :]
            density += block.astype(jnp.bfloat16).astype(jnp.float32)
        return density

    loads[6].wait()
    density = charge_ref[...]
    if ngy <= 4:
        for source in range(ngy):
            density = deposit(source, density)
    else:
        density = lax.fori_loop(0, ngy, deposit, density)
    g = four_pi * density

    wait_faces(0, eps_ref, False)

    def halo(kind):
        return tuple((buffer[kind, 0], buffer[kind, 1]) for buffer in halos)

    eps_around = around(eps, halo(0))
    weight_sum = 0.5 * (6.0 * eps + sum(eps_around[1:], eps_around[0]))
    weights = [0.5 * (eps + other) for other in eps_around]
    inverse = relax_weight / weight_sum
    f = inverse * g
    f_ref[...] = f
    send_faces(1, f_ref)

    each(n, lambda k: gather_copy(0, k).wait_recv())
    nx1, ny1 = 2 * whole1.shape[0], whole1.shape[1]

    def down_y(values):
        rows = ny1 // 2
        parts = []
        for c in range(ngz):
            half2[c] = values[:, :, c * cz : (c + 1) * cz]
            parts.append(half2[c, :, pl.ds(0, rows, stride=2), :] + half2[c, :, pl.ds(1, rows, stride=2), :])
        return jnp.concatenate(parts, 2)

    def pair_sum_y(values):
        low = iota(values.shape, 1) % 2 == 0
        return values + jnp.where(low, rolled(values, -1, 1), rolled(values, 1, 1))

    def restrict_1(values):
        return 0.125 * down_y(pair_sum_z(pair_sum_x(values), 2))

    def restrict_2(values):
        return 0.125 * pair_sum_y(pair_sum_z(pair_sum_x(values), 4))

    eps1 = assemble(0)
    eps2 = restrict_1(eps1)
    eps3 = restrict_2(eps2)
    level1, level2, level3 = Coarse(eps1, 1, 1, 2), Coarse(eps2, 2, 1, 4), Coarse(eps3, 3, 2, 8)

    wait_faces(1, f_ref, False)

    def beside(values, halo_values):
        total = None
        for weight, other in zip(weights, around(values, halo_values)):
            total = weight * other if total is None else total + weight * other
        return total

    f_halo = halo(1)
    gather_ref[1, me] = packed(restrict((1.0 / 3.0) * g + beside(f, f_halo)))
    each(n, lambda k: gather_copy(1, k).start())
    each(n, lambda k: gather_copy(1, k).wait_recv())

    g1 = assemble(1)
    f1 = level1.first(g1)
    g2 = restrict_1(level1.residual_of_first(g1, f1))
    f2 = level2.first(g2)
    g3 = restrict_2(level2.residual_of_first(g2, f2))
    f3 = level3.first(g3)
    for _ in range(NU_COARSE - 1):
        f3 = level3.sweep(g3, f3)
    f2 = level2.sweep(g2, f2 + repeat_x(f3))
    fine2 = repeat_x(f2)
    for c in range(ngz):
        for odd in range(2):
            up1[c, :, pl.ds(odd, ny1 // 2, stride=2), :] = fine2[:, :, c * cz : (c + 1) * cz]
    f1 = level1.sweep(g1, f1 + jnp.concatenate([up1[c] for c in range(ngz)], 2))
    for c in range(ngz):
        for odd in range(2):
            up0[c + 1, 1 : nx1 + 1, pl.ds(cy + odd, ny1, stride=2), :] = f1[:, :, c * cz : (c + 1) * cz]

    def part(dx, lx, dy, dz):
        return up0[gz + dz, pl.ds(gx * bx + dx, lx), pl.ds(pl.multiple_of((gy + dy) * cy, cy), cy), :]

    (xl, xh), (yl, yh), (zl, zh) = f_halo
    f = f + repeat_x(part(1, bx, 1, 1))
    f_halo = (
        (xl + part(0, 1, 1, 1)[0], xh + part(bx + 1, 1, 1, 1)[0]),
        (yl + repeat_x(part(1, bx, 0, 1)[:, cy - 1 : cy, :]), yh + repeat_x(part(1, bx, 2, 1)[:, 0:1, :])),
        (zl + repeat_x(part(1, bx, 1, 0)), zh + repeat_x(part(1, bx, 1, 2))),
    )
    out_ref[...] = (1.0 / 3.0) * f + inverse * (g + beside(f, f_halo))

    each(ngy, lambda k: ion_copy(k).wait_send())
    wait_faces(0, eps_ref, True)
    wait_faces(1, f_ref, True)
    each(n, lambda k: gather_copy(0, k).wait_send())
    each(n, lambda k: gather_copy(1, k).wait_send())


def solution(mesh):
    ngx, ngy, ngz = mesh.shape["gx"], mesh.shape["gy"], mesh.shape["gz"]

    def per_device(charge_density, permittivity, ion_centers, ion_widths, ion_charges, block_counts, block_anchors):
        cx, cy, cz = charge_density.shape
        n = ngx * ngy * ngz
        nx1, ny1 = ngx * cx // 2, ngy * cy // 2
        f32 = jnp.float32
        dma = pltpu.SemaphoreType.DMA
        return pl.pallas_call(
            functools.partial(kernel, (ngx, ngy, ngz)),
            out_shape=pltpu.VMEM((cx, cy, cz), f32),
            in_specs=[pl.BlockSpec(memory_space=pltpu.HBM)] * 7,
            out_specs=pl.BlockSpec(memory_space=pltpu.VMEM),
            scratch_shapes=[
                pltpu.VMEM((cx, cy, cz), f32),
                pltpu.VMEM((cx, cy, cz), f32),
                pltpu.VMEM((3, ngy, CAP), f32),
                pltpu.VMEM((ngy, CAP), f32),
                pltpu.VMEM((ngy, CAP), f32),
                pltpu.VMEM((1, ngy), jnp.int32),
                pltpu.VMEM((3, ngy, CAP), jnp.int32),
                dma((7,)),
                pltpu.VMEM((cx, cy, cz), f32),
                pltpu.VMEM((2, 2, cy, cz), f32),
                pltpu.VMEM((2, 2, cx, 1, cz), f32),
                pltpu.VMEM((2, 2, cx, cy, cz), f32),
                pltpu.VMEM((2, 2, cx, 1, cz), f32),
                pltpu.VMEM((cx // 2, cy, cz), f32),
                pltpu.VMEM((2, n, cx // 4, cy // 2, cz), f32),
                pltpu.VMEM((ngy, 8, 128), f32),
                pltpu.VMEM((ngy, 8, 128), f32),
                pltpu.VMEM((nx1 // 2, ny1, ngz * cz), f32),
                pltpu.VMEM((ngz, nx1 // 2, ny1, cz), f32),
                pltpu.VMEM((ngz, nx1, ny1, cz), f32),
                pltpu.VMEM((ngz + 2, nx1 + 2, (ngy + 2) * cy, cz), f32),
                dma((12,)), dma((12,)), dma((2, n)), dma((2, n)), dma((ngy,)), dma((ngy,)),
            ],
            compiler_params=pltpu.CompilerParams(
                collective_id=0, has_side_effects=True, vmem_limit_bytes=65408 * 1024),
        )(
            charge_density,
            permittivity,
            ion_centers.reshape(3, ngy, CAP),
            ion_widths.reshape(ngy, CAP),
            ion_charges.reshape(ngy, CAP),
            block_counts.reshape(1, ngy),
            block_anchors.reshape(3, ngy, CAP),
        )

    field = P(("groups", "gx"), "gy", "gz")
    return jax.shard_map(
        per_device, mesh=mesh, in_specs=(field,) * 7, out_specs=field, check_vma=False)
```

```python
import functools
import math

import jax
import jax.numpy as jnp
from jax import lax
from jax.experimental import pallas as pl
from jax.experimental.pallas import tpu as pltpu
from jax.sharding import PartitionSpec as P

PATCH = 8
CAP = 8
NU_COARSE = 8
MESH = pl.DeviceIdType.MESH

four_pi = 4.0 * math.pi
relax_weight = 2.0 / 3.0
gauss_norm = (2.0 * math.pi) ** 1.5


def iota(shape, dim):
    return lax.broadcasted_iota(jnp.int32, shape, dim)


def each(count, body):
    if count <= 16:
        for k in range(1, count):
            body(k)
    else:
        lax.fori_loop(1, count, lambda k, c: (body(k), c)[1], 0)


def rolled(values, step, dim):
    return pltpu.roll(values, step % values.shape[dim], dim)


def pair_sum_z(values, step):
    low = (iota(values.shape, 2) // step) % 2 == 0
    return values + jnp.where(low, rolled(values, -step, 2), rolled(values, step, 2))


def pair_sum_x(values):
    a, b, c = values.shape
    v = values.reshape(a // 2, 2, b, c)
    return v[:, 0] + v[:, 1]


def repeat_x(values):
    a, b, c = values.shape
    return jnp.broadcast_to(values[:, None], (a, 2, b, c)).reshape(2 * a, b, c)


def shifted_x(values, step):
    zero = jnp.zeros_like(values[:1])
    if step > 0:
        return jnp.concatenate([values[1:], zero], 0)
    return jnp.concatenate([zero, values[:-1]], 0)


def packed(values):
    a, b, c = values.shape
    v = values.reshape(a // 2, 2, b, c)
    return jnp.where(iota((a // 2, b, c), 2) % 2 == 0, v[:, 0], v[:, 1])


def unpacked(values):
    a, b, c = values.shape
    even = iota(values.shape, 2) % 2 == 0
    first = jnp.where(even, values, rolled(values, 1, 2))
    second = jnp.where(even, rolled(values, -1, 2), values)
    return jnp.stack([first, second], 1).reshape(2 * a, b, c)


class Coarse:
    def __init__(self, eps, level, sy, sz):
        self.sy, self.sz = sy, sz
        self.spacing = 1.0 / 4.0**level
        y, z = iota(eps.shape, 1), iota(eps.shape, 2)
        ny, nz = eps.shape[1], eps.shape[2]
        xp, xm = shifted_x(eps, 1), shifted_x(eps, -1)
        in_y, in_z = y < ny - sy, z < nz - sz
        yp = jnp.where(in_y, rolled(eps, -sy, 1), 0.0)
        ym = jnp.where(y >= sy, rolled(eps, sy, 1), 0.0)
        zp = jnp.where(in_z, rolled(eps, -sz, 2), 0.0)
        zm = jnp.where(z >= sz, rolled(eps, sz, 2), 0.0)
        weight_sum = 0.5 * (6.0 * eps + xp + xm + yp + ym + zp + zm)
        self.inverse = (relax_weight / self.spacing) / weight_sum
        self.wx = 0.5 * (eps + xp)
        self.wy = jnp.where(in_y, 0.5 * (eps + yp), 0.0)
        self.wz = jnp.where(in_z, 0.5 * (eps + zp), 0.0)

    def beside(self, f):
        out = self.wx * shifted_x(f, 1) + shifted_x(self.wx * f, -1)
        out += self.wy * rolled(f, -self.sy, 1) + rolled(self.wy * f, self.sy, 1)
        out += self.wz * rolled(f, -self.sz, 2) + rolled(self.wz * f, self.sz, 2)
        return self.spacing * out

    def first(self, g):
        return self.inverse * g

    def residual_of_first(self, g, f):
        return (1.0 / 3.0) * g + self.beside(f)

    def sweep(self, g, f):
        return (1.0 / 3.0) * f + self.inverse * (g + self.beside(f))


def around(values, halo):
    (xl, xh), (yl, yh), (zl, zh) = halo
    y, z = iota(values.shape, 1), iota(values.shape, 2)
    ny, nz = values.shape[1], values.shape[2]
    shape = values.shape
    return (
        jnp.concatenate([values[1:], xh[None]], 0),
        jnp.concatenate([xl[None], values[:-1]], 0),
        jnp.where(y == ny - 1, jnp.broadcast_to(yh, shape), rolled(values, -1, 1)),
        jnp.where(y == 0, jnp.broadcast_to(yl, shape), rolled(values, 1, 1)),
        jnp.where(z == nz - 1, rolled(zh, -1, 2), rolled(values, -1, 2)),
        jnp.where(z == 0, rolled(zl, 1, 2), rolled(values, 1, 2)),
    )


def kernel(
    sizes,
    charge_in, eps_in, centers_in, widths_in, charges_in, counts_in, anchors_in,
    out_ref,
    charge_ref, eps_ref, centers_ref, widths_ref, charges_ref, counts_ref, anchors_ref, load_sem,
    f_ref, hx_ref, hy_ref, hz_ref, sy_ref, pairs_ref, gather_ref, ions_out, ions_in, whole1, half2, up1, up0,
    face_send, face_recv, gather_send, gather_recv, ion_send, ion_recv,
):
    ngx, ngy, ngz = sizes
    cx, cy, cz = charge_ref.shape
    bx, by, hx = cx // 2, cy // 2, cx // 4
    n = ngx * ngy * ngz
    gx, gy, gz = lax.axis_index("gx"), lax.axis_index("gy"), lax.axis_index("gz")
    me = (gx * ngy + gy) * ngz + gz

    def peer(k):
        at = (me + k) % n
        return {"gx": at // (ngy * ngz), "gy": (at // ngz) % ngy, "gz": at % ngz}

    loads = [
        pltpu.make_async_copy(source, target, load_sem.at[index])
        for index, (source, target) in enumerate((
            (eps_in, eps_ref), (counts_in, counts_ref), (centers_in, centers_ref), (widths_in, widths_ref),
            (charges_in, charges_ref), (anchors_in, anchors_ref), (charge_in, charge_ref)))
    ]
    for load in loads:
        load.start()
    barrier = pltpu.get_barrier_semaphore()
    each(n, lambda k: pl.semaphore_signal(barrier, inc=1, device_id=peer(k), device_id_type=MESH))

    axes = (("gx", gx, ngx), ("gy", gy, ngy), ("gz", gz, ngz))
    halos = (hx_ref, hy_ref, hz_ref)
    for axis in range(3):
        name, at, count = axes[axis]
        for side, missing in ((0, at == 0), (1, at == count - 1)):
            @pl.when(missing)
            def _(axis=axis, side=side):
                for kind in range(2):
                    buffer = halos[axis].at[kind, side]
                    buffer[...] = jnp.zeros(buffer.shape, jnp.float32)

    def face_copy(kind, axis, side, source):
        name, at, count = axes[axis]
        target = at + 1 if side == 0 else at - 1
        index = (kind * 3 + axis) * 2 + side
        return pltpu.make_async_remote_copy(
            src_ref=source, dst_ref=halos[axis].at[kind, side],
            send_sem=face_send.at[index], recv_sem=face_recv.at[index],
            device_id={name: target}, device_id_type=MESH)

    def face_sources(kind, field):
        return (
            (field.at[cx - 1], field.at[0]),
            (sy_ref.at[kind, 0], sy_ref.at[kind, 1]),
            (field, field),
        )

    def send_faces(kind, field):
        sy_ref[kind, 0] = field[:, cy - 1 : cy, :]
        sy_ref[kind, 1] = field[:, 0:1, :]
        sources = face_sources(kind, field)
        for axis in range(3):
            at, count = axes[axis][1:]
            for side in range(2):
                @pl.when((at < count - 1) if side == 0 else (at > 0))
                def _(axis=axis, side=side):
                    face_copy(kind, axis, side, sources[axis][side]).start()

    def wait_faces(kind, field, sent):
        sources = face_sources(kind, field)
        for axis in range(3):
            at, count = axes[axis][1:]
            for side in range(2):
                up = (side == 0) == sent
                @pl.when((at < count - 1) if up else (at > 0))
                def _(axis=axis, side=side):
                    copy = face_copy(kind, axis, side, sources[axis][side])
                    copy.wait_send() if sent else copy.wait_recv()

    def gather_copy(kind, k):
        return pltpu.make_async_remote_copy(
            src_ref=gather_ref.at[kind, me], dst_ref=gather_ref.at[kind, me],
            send_sem=gather_send.at[kind], recv_sem=gather_recv.at[kind],
            device_id=peer(k), device_id_type=MESH)

    def wait_gather(kind, semaphore):
        blocks = gather_ref.at[kind, pl.ds(0, n - 1)]
        pltpu.make_async_copy(blocks, blocks, semaphore.at[kind]).wait()

    def ion_copy(k):
        to = (gy + k) % ngy
        return pltpu.make_async_remote_copy(
            src_ref=ions_out.at[to], dst_ref=ions_in.at[gy],
            send_sem=ion_send.at[k], recv_sem=ion_recv.at[k],
            device_id={"gy": to}, device_id_type=MESH)

    def restrict(values):
        pairs_ref[...] = pair_sum_z(pair_sum_x(values), 1)
        return 0.125 * (pairs_ref[:, pl.ds(0, by, stride=2), :] + pairs_ref[:, pl.ds(1, by, stride=2), :])

    def assemble(kind):
        for a in range(ngx):
            for b in range(ngy):
                for c in range(ngz):
                    whole1[a * hx : (a + 1) * hx, b * by : (b + 1) * by, c * cz : (c + 1) * cz] = gather_ref[
                        kind, (a * ngy + b) * ngz + c]
        return unpacked(whole1[...])

    up0[...] = jnp.zeros_like(up0)
    loads[0].wait()
    eps = eps_ref[...]
    gather_ref[0, me] = packed(restrict(eps))
    for load in loads[1:6]:
        load.wait()
    counts = counts_ref[...]
    for d in range(ngy):
        for c in range(3):
            ions_out[d, c : c + 1, 0:CAP] = centers_ref[c, d : d + 1, :]
        ions_out[d, 3:4, 0:CAP] = widths_ref[d : d + 1, :]
        live = iota((1, CAP), 1) < jnp.broadcast_to(counts[:, d : d + 1], (1, CAP))
        ions_out[d, 4:5, 0:CAP] = jnp.where(live, charges_ref[d : d + 1, :], 0.0)
        ions_out[d, 5:6, 0:CAP] = anchors_ref[2, d : d + 1, :].astype(jnp.float32)
        ions_out[d, 6:8, 0:CAP] = jnp.zeros((2, CAP), jnp.float32)
        ions_out[d, :, CAP:] = jnp.ones((8, 128 - CAP), jnp.float32)
    ions_in[gy] = ions_out[gy]

    pl.semaphore_wait(barrier, n - 1)
    each(ngy, lambda k: ion_copy(k).start())
    send_faces(0, eps_ref)
    each(n, lambda k: gather_copy(0, k).start())

    each(ngy, lambda k: ion_copy(k).wait_recv())

    def deposit(source, density):
        tile = ions_in[source]
        lines = tile.T[0:CAP]
        u, v, s, q = tile[0:1], tile[1:2], tile[3:4], tile[4:5]
        decay = 0.5 / (s * s)
        amplitude = q / (gauss_norm * s * s * s)
        j = iota((cy, 128), 0).astype(jnp.float32)
        along_y = jnp.exp(-((j - v) ** 2) * decay)
        flat = jnp.stack(
            [(amplitude * jnp.exp(-((float(i) - u) ** 2) * decay)) * along_y for i in range(cx)])
        w, spread, anchor = lines[:, 2:3], lines[:, 3:4], lines[:, 5:6]
        position = iota((CAP, cz), 1).astype(jnp.float32) - anchor
        along_z = jnp.exp(-((position - w) ** 2) * (0.5 / (spread * spread)))
        along_z = jnp.where((position >= 0.0) & (position < float(PATCH)), along_z, 0.0)
        for e in range(CAP):
            block = flat[:, :, e : e + 1] * along_z[None, e : e + 1, :]
            density += block.astype(jnp.bfloat16).astype(jnp.float32)
        return density

    loads[6].wait()
    density = charge_ref[...]
    if ngy <= 4:
        for source in range(ngy):
            density = deposit(source, density)
    else:
        density = lax.fori_loop(0, ngy, deposit, density)
    g = four_pi * density

    wait_faces(0, eps_ref, False)

    def halo(kind):
        return tuple((buffer[kind, 0], buffer[kind, 1]) for buffer in halos)

    eps_around = around(eps, halo(0))
    weight_sum = 0.5 * (6.0 * eps + sum(eps_around[1:], eps_around[0]))
    weights = [0.5 * (eps + other) for other in eps_around]
    inverse = relax_weight / weight_sum
    f = inverse * g
    f_ref[...] = f
    send_faces(1, f_ref)

    wait_gather(0, gather_recv)
    nx1, ny1 = 2 * whole1.shape[0], whole1.shape[1]

    def down_y(values):
        rows = ny1 // 2
        parts = []
        for c in range(ngz):
            half2[c] = values[:, :, c * cz : (c + 1) * cz]
            parts.append(half2[c, :, pl.ds(0, rows, stride=2), :] + half2[c, :, pl.ds(1, rows, stride=2), :])
        return jnp.concatenate(parts, 2)

    def pair_sum_y(values):
        low = iota(values.shape, 1) % 2 == 0
        return values + jnp.where(low, rolled(values, -1, 1), rolled(values, 1, 1))

    def restrict_1(values):
        return 0.125 * down_y(pair_sum_z(pair_sum_x(values), 2))

    def restrict_2(values):
        return 0.125 * pair_sum_y(pair_sum_z(pair_sum_x(values), 4))

    eps1 = assemble(0)
    eps2 = restrict_1(eps1)
    eps3 = restrict_2(eps2)
    level1, level2, level3 = Coarse(eps1, 1, 1, 2), Coarse(eps2, 2, 1, 4), Coarse(eps3, 3, 2, 8)

    wait_faces(1, f_ref, False)

    def beside(values, halo_values):
        total = None
        for weight, other in zip(weights, around(values, halo_values)):
            total = weight * other if total is None else total + weight * other
        return total

    f_halo = halo(1)
    gather_ref[1, me] = packed(restrict((1.0 / 3.0) * g + beside(f, f_halo)))
    each(n, lambda k: gather_copy(1, k).start())
    each(ngy, lambda k: ion_copy(k).wait_send())
    wait_faces(0, eps_ref, True)
    wait_faces(1, f_ref, True)
    wait_gather(0, gather_send)
    wait_gather(1, gather_send)
    wait_gather(1, gather_recv)

    g1 = assemble(1)
    f1 = level1.first(g1)
    g2 = restrict_1(level1.residual_of_first(g1, f1))
    f2 = level2.first(g2)
    g3 = restrict_2(level2.residual_of_first(g2, f2))
    f3 = level3.first(g3)
    for _ in range(NU_COARSE - 1):
        f3 = level3.sweep(g3, f3)
    f2 = level2.sweep(g2, f2 + repeat_x(f3))
    fine2 = repeat_x(f2)
    for c in range(ngz):
        for odd in range(2):
            up1[c, :, pl.ds(odd, ny1 // 2, stride=2), :] = fine2[:, :, c * cz : (c + 1) * cz]
    f1 = level1.sweep(g1, f1 + jnp.concatenate([up1[c] for c in range(ngz)], 2))
    for c in range(ngz):
        for odd in range(2):
            up0[c + 1, 1 : nx1 + 1, pl.ds(cy + odd, ny1, stride=2), :] = f1[:, :, c * cz : (c + 1) * cz]

    def part(dx, lx, dy, dz):
        return up0[gz + dz, pl.ds(gx * bx + dx, lx), pl.ds(pl.multiple_of((gy + dy) * cy, cy), cy), :]

    (xl, xh), (yl, yh), (zl, zh) = f_halo
    f = f + repeat_x(part(1, bx, 1, 1))
    f_halo = (
        (xl + part(0, 1, 1, 1)[0], xh + part(bx + 1, 1, 1, 1)[0]),
        (yl + repeat_x(part(1, bx, 0, 1)[:, cy - 1 : cy, :]), yh + repeat_x(part(1, bx, 2, 1)[:, 0:1, :])),
        (zl + repeat_x(part(1, bx, 1, 0)), zh + repeat_x(part(1, bx, 1, 2))),
    )
    out_ref[...] = (1.0 / 3.0) * f + inverse * (g + beside(f, f_halo))


def solution(mesh):
    ngx, ngy, ngz = mesh.shape["gx"], mesh.shape["gy"], mesh.shape["gz"]

    def per_device(charge_density, permittivity, ion_centers, ion_widths, ion_charges, block_counts, block_anchors):
        cx, cy, cz = charge_density.shape
        n = ngx * ngy * ngz
        nx1, ny1 = ngx * cx // 2, ngy * cy // 2
        f32 = jnp.float32
        dma = pltpu.SemaphoreType.DMA
        return pl.pallas_call(
            functools.partial(kernel, (ngx, ngy, ngz)),
            out_shape=pltpu.VMEM((cx, cy, cz), f32),
            in_specs=[pl.BlockSpec(memory_space=pltpu.HBM)] * 7,
            out_specs=pl.BlockSpec(memory_space=pltpu.VMEM),
            scratch_shapes=[
                pltpu.VMEM((cx, cy, cz), f32),
                pltpu.VMEM((cx, cy, cz), f32),
                pltpu.VMEM((3, ngy, CAP), f32),
                pltpu.VMEM((ngy, CAP), f32),
                pltpu.VMEM((ngy, CAP), f32),
                pltpu.VMEM((1, ngy), jnp.int32),
                pltpu.VMEM((3, ngy, CAP), jnp.int32),
                dma((7,)),
                pltpu.VMEM((cx, cy, cz), f32),
                pltpu.VMEM((2, 2, cy, cz), f32),
                pltpu.VMEM((2, 2, cx, 1, cz), f32),
                pltpu.VMEM((2, 2, cx, cy, cz), f32),
                pltpu.VMEM((2, 2, cx, 1, cz), f32),
                pltpu.VMEM((cx // 2, cy, cz), f32),
                pltpu.VMEM((2, n, cx // 4, cy // 2, cz), f32),
                pltpu.VMEM((ngy, 8, 128), f32),
                pltpu.VMEM((ngy, 8, 128), f32),
                pltpu.VMEM((nx1 // 2, ny1, ngz * cz), f32),
                pltpu.VMEM((ngz, nx1 // 2, ny1, cz), f32),
                pltpu.VMEM((ngz, nx1, ny1, cz), f32),
                pltpu.VMEM((ngz + 2, nx1 + 2, (ngy + 2) * cy, cz), f32),
                dma((12,)), dma((12,)), dma((2,)), dma((2,)), dma((ngy,)), dma((ngy,)),
            ],
            compiler_params=pltpu.CompilerParams(
                collective_id=0, has_side_effects=True, vmem_limit_bytes=65408 * 1024),
        )(
            charge_density,
            permittivity,
            ion_centers.reshape(3, ngy, CAP),
            ion_widths.reshape(ngy, CAP),
            ion_charges.reshape(ngy, CAP),
            block_counts.reshape(1, ngy),
            block_anchors.reshape(3, ngy, CAP),
        )

    field = P(("groups", "gx"), "gy", "gz")
    return jax.shard_map(
        per_device, mesh=mesh, in_specs=(field,) * 7, out_specs=field, check_vma=False)
```
